512 devices in a mesh: group: 16 (over z_lo, x, core), shard: 32 (over z_hi, y).
Axes of the slice: x: 4, y: 8, z: 8 (z_hi: 4, z_lo: 2; z = z_hi * 2 + z_lo), core: 2. Of those that a mesh axis runs over, the one named last changes fastest.
Arguments:
- master_new: float32 [32, 96, 128, 128], P('shard', 'group'), may hold values from -60 to 60
- sent_base: bfloat16 [32, 96, 128, 128], P('shard', 'group'), may hold values from -6 to 6
- rollout_base: bfloat16 [12288, 2048], P('shard'), may hold values from -6 to 6
- tokens: bfloat16 [16, 32, 256, 2048], P('group', 'shard'), may hold values from -0.13183594 to 0.13183594
- lengths: int32 [32, 16], replicated, may hold values from 1 to 6, 48 in all within a row
- expert_slot: int32 [8], replicated, may hold values from 0 to 7, each once
Outputs:
- new_weights: bfloat16 [12288, 2048], P('shard')
- in_flight: bfloat16 [16, 32, 256, 384], P('group', 'shard')
The draws below stay inside these ranges and needn't reach their ends.
Inputs may be any that keep to these rules, and one draw needn't show every extreme that they name: `lengths`: row s splits column s's 48 tiles among the 16 groups; each row sums to 48 and its largest entry is 6. `expert_slot`: a permutation of the 8 slots.
All inputs are finite; a program needn't handle non-finite values.
Results may differ from the reference program's by a relative error of at most 0.0051.
Values may be sent and summed in bfloat16 or wider, within the bound.
No kernel may reach another device: no remote copies, remote signals or barrier semaphores. Data moves between devices by JAX's collectives and lax.ppermute only.
A program may use at most 64 MiB of HBM per device.

```python
import math
import jax
import jax.numpy as jnp
import numpy as np
from jax import lax

MI = 1536
DW = 2048
BLK = 128
TPW = 4
TOK = 256
EXPERTS = 8
ROWS_DEV = 384
STRETCH = 48
MOST = 6
N_GROUP = 16
N_SHARD = 32


def draw_master_new(key, part):
    key = jax.random.fold_in(key, 11)
    key_values, key_rows, key_cols = jax.random.split(key, 3)
    shape = (N_SHARD, N_GROUP * MOST, BLK, BLK)
    span = math.log(3.2)
    row_scale = jnp.exp(jax.random.uniform(key_rows, (N_SHARD, N_GROUP * MOST, BLK, 1), jnp.float32, 0.0, span))
    col_scale = jnp.exp(jax.random.uniform(key_cols, (N_SHARD, N_GROUP * MOST, 1, BLK), jnp.float32, 0.0, span))
    values = jax.random.normal(key_values, shape, jnp.float32)
    return jnp.clip(values * row_scale * col_scale, -60.0, 60.0)


def steps_of(rng, shape, shards, low, top_value):
    def one(position, blocks):
        heights = jax.random.uniform(jax.random.fold_in(jax.random.fold_in(rng, 6), position), (blocks,), jnp.float32, low / len(shards), top_value / len(shards))
        return jnp.repeat(jnp.exp(heights), shape[position] // blocks).reshape((-1,) + (1,) * (len(shape) - position - 1))

    gain = one(*shards[0])
    for cut in shards[1:]:
        gain = gain * one(*cut)
    return gain


def split_up(number_of, total, reach, skew):
    loads = [(1 << 20) // math.isqrt(standing ** skew) + 1 for standing in range(2, number_of + 1)]
    spare, given = total - reach - (number_of - 1), [1] * (number_of - 1)
    while spare > 0:
        candidates = [i for i in range(number_of - 1) if given[i] < reach]
        pool, remaining = sum([loads[i] for i in candidates]), spare
        for i in candidates:
            extra = min(reach - given[i], max(1, remaining * loads[i] // pool), spare)
            given[i] = given[i] + extra
            spare = spare - extra
    return np.array([reach] + given)


def ragged_sizes(key, count, total, most, slope):
    if count == 2:
        one = jax.random.randint(key, (), max(1, total - most), min(most, total - 1) + 1)
        return jnp.stack([one, total - one])
    sizes = jnp.asarray(split_up(count, total, most, slope), jnp.int32)
    couples = (count - 1) // 2
    giver, sink = sizes[1:1 + 2 * couples:2], sizes[2:2 + 2 * couples:2]
    margin = jnp.minimum(giver - 1, most - sink)
    shifted = jax.random.randint(jax.random.fold_in(key, 1), (couples,), 0, 1 << 20) % (margin + 1)
    sizes = sizes.at[1:1 + 2 * couples:2].set(giver - shifted).at[2:2 + 2 * couples:2].set(sink + shifted)
    return sizes[jax.random.permutation(jax.random.fold_in(key, 2), count)]


def bell_draw(rng, shape, spread, reach, pieces=(), kind=jnp.bfloat16):
    level = steps_of(rng, shape, pieces, -0.22, 0.18) if pieces else 1.0
    drawn = jax.random.normal(rng, shape, jnp.float32) * spread * level
    return jnp.minimum(jnp.maximum(drawn, -reach), reach).astype(kind)


def setup_inputs(seed: int = 0) -> dict:
    streams_of = jax.random.split(jax.random.key(seed), 7)
    return {
        "master_new": draw_master_new(jax.random.fold_in(streams_of[6], 71), 0),
        "sent_base": bell_draw(streams_of[1], (N_SHARD, N_GROUP * MOST, BLK, BLK), 1.0, 6.0, ((0, 32), (1, 16))),
        "rollout_base": bell_draw(streams_of[2], (EXPERTS * MI, DW), 1.0, 6.0, ((0, 32),)),
        "tokens": bell_draw(streams_of[3], (N_GROUP, N_SHARD, TOK, DW), (DW ** -0.5), 0.13183594, ((0, 16), (1, 32))),
        "lengths": jax.vmap(lambda own: ragged_sizes(own, N_GROUP, STRETCH, MOST, 2))(jax.random.split(streams_of[4], N_SHARD)).reshape((N_SHARD, N_GROUP)).astype(jnp.int32),
        "expert_slot": jax.random.permutation(streams_of[5], EXPERTS).astype(jnp.int32),
    }


CLIP_RATIO = 2.5
EPSILON = 1e-06

def encode(master, previous):
    change = master - previous.astype(jnp.float32)
    tile_scale = jnp.sqrt(lax.optimization_barrier(jnp.mean(change * change, axis=(-2, -1))) + EPSILON).astype(jnp.bfloat16)
    tile_scale = lax.optimization_barrier(tile_scale)
    widened = tile_scale.astype(jnp.float32)[..., None, None]
    encoded = jnp.clip(change / widened, -CLIP_RATIO, CLIP_RATIO).astype(jnp.bfloat16)
    return (encoded, tile_scale)

def decode(encoded, tile_scale):
    encoded = lax.optimization_barrier(encoded)
    return encoded.astype(jnp.float32) * tile_scale.astype(jnp.float32)[..., None, None]

def reference(master_new, sent_base, rollout_base, tokens, lengths, expert_slot):
    tile_rows = MI // BLK
    tile_cols = DW // BLK
    per_stretch = tile_rows * tile_cols // TPW
    encoded, tile_scale = encode(master_new, sent_base)
    run_ends = jnp.cumsum(lengths, axis=1).astype(jnp.int32)
    starts = (run_ends - lengths).astype(jnp.int32)
    positions = jnp.arange(per_stretch, dtype=jnp.int32)
    owners = lax.optimization_barrier(jnp.sum((run_ends[:, None, :] <= positions[None, :, None]).astype(jnp.int32), axis=2)).astype(jnp.int32)
    sources = (owners * MOST + positions[None, :] - jnp.take_along_axis(starts, owners, axis=1)).astype(jnp.int32)
    stretch_tiles = jnp.take_along_axis(encoded, sources[:, :, None, None], axis=1)
    stretch_scale = jnp.take_along_axis(tile_scale, sources, axis=1)
    decoded = decode(stretch_tiles, stretch_scale)
    expert_grid = decoded.reshape(tile_cols, EXPERTS, tile_rows, BLK, BLK)
    expert_grid = expert_grid.transpose(1, 2, 3, 0, 4).reshape(EXPERTS, MI, DW)
    placed = jnp.zeros_like(expert_grid).at[expert_slot].set(expert_grid)
    refreshed = rollout_base.astype(jnp.float32).reshape(EXPERTS, MI, DW) + placed
    new_weights = refreshed.astype(jnp.bfloat16).reshape(EXPERTS * MI, DW)
    base_slabs = rollout_base.astype(jnp.float32).reshape(N_SHARD, ROWS_DEV, DW)

    def project(group_tokens):
        return jnp.einsum('std,srd->str', group_tokens.astype(jnp.float32), base_slabs).astype(jnp.bfloat16)
    in_flight = lax.map(project, tokens)
    return (new_weights, in_flight)
```

```python
import jax
import jax.numpy as jnp
from jax import lax
from jax.experimental import pallas as pl
from jax.experimental.pallas import tpu as pltpu
from jax.sharding import Mesh
from jax.sharding import PartitionSpec as P

CLIP_RATIO = 2.5
EPSILON = 1e-06

BLK = 128
HALF = 4
TROWS = 12
MOST = 6
GROUPS = 16


def place():
    zl, x, c = lax.axis_index("zl"), lax.axis_index("x"), lax.axis_index("c")
    zh, y = lax.axis_index("zh"), lax.axis_index("y")
    return zl, x, c, zh, y


def mod16(v):
    return lax.bitwise_and(v, 15)


def encode_kernel(lengths, master, sent, out):
    zl, x, c, zh, y = place()
    g, s = zl * 8 + x * 2 + c, zh * 8 + y
    start = jnp.int32(0)
    for i in range(GROUPS):
        start += jnp.where(i < g, lengths[s, i], 0)
    count = lengths[s, g]
    for j in range(MOST):
        change = master[0, j] - sent[0, j].astype(jnp.float32)
        mean = jnp.sum(change * change, axis=(0, 1), keepdims=True) * (1.0 / (BLK * BLK))
        scale = jnp.sqrt(mean + EPSILON).astype(jnp.bfloat16).astype(jnp.float32)
        encoded = jnp.clip(change / scale, -CLIP_RATIO, CLIP_RATIO).astype(jnp.bfloat16)
        value = (encoded.astype(jnp.float32) * scale).astype(jnp.bfloat16)

        @pl.when(j < count)
        def _():
            out[mod16(start + j + 4 * (y // 2) + zh)] = value


def to_y_kernel(lengths, slots, got, out):
    zl, x, c, zh, y = place()
    g, s = zl * 8 + x * 2 + c, zh * 8 + y
    first = mod16(g - 4 * (y // 2) - zh + 32)
    owners = [jnp.int32(0)] * 3
    end = jnp.int32(0)
    for i in range(GROUPS - 1):
        end += lengths[s, i]
        for m in range(3):
            owners[m] += jnp.where(end <= first + 16 * m, 1, 0)
    for m in range(3):
        q = first + 16 * m
        slot = slots[HALF * (y % 2) + q // TROWS]
        out[(slot % 2) * 4 + (q % TROWS) // 3] = got[owners[m]]


def expert_at(slots, p):
    e = jnp.int32(0)
    for i in range(2 * HALF):
        e += jnp.where(slots[i] == p, i, 0)
    return e


def to_z_kernel(slots, got, out):
    zl, x, c, zh, y = place()
    g = zl * 8 + x * 2 + c
    for to in range(4):
        e = expert_at(slots, 2 * to + y // 4)
        u = mod16(g - 12 * (e % HALF) - 3 * (y % 4) - zh + 64)
        tile = got[(u // 4) * 2 + e // HALF]
        out[2 * to] = tile
        out[2 * to + 1] = tile


def hole(x, c, y):
    return lax.bitwise_and(2 * x + c - 3 * (y % 4) - 3 + 16, 3)


def to_x_kernel(got, out):
    zl, x, c, zh, y = place()
    skip = hole(x, c, y)
    for a in range(3):
        at = lax.bitwise_and(skip + 1 + a, 3)
        for lo in range(2):
            tile = got[at * 2 + lo]
            for to in range(4):
                out[to * 6 + a * 2 + lo] = tile


def add_kernel(slots, mine, other, base, out):
    zl, x, c, zh, y = place()
    e4 = expert_at(slots, 2 * zh + y // 4) % HALF
    for i in range(3):
        for col in range(16):
            from_zh = col // 4
            g = mod16(i + 4 * (col % 4) + 12 * e4 + 3 * (y % 4) + from_zh)
            from_zl, from_x, from_c = g // 8, (g // 2) % 4, g % 2
            a = lax.bitwise_and(from_zh - hole(from_x, from_c, y) - 1 + 8, 3)
            n = from_x * 6 + a * 2 + from_zl
            tile = jnp.where(from_c == c, mine[n], other[n]).astype(jnp.float32)
            rows, cols = pl.ds(i * BLK, BLK), pl.ds(col * BLK, BLK)
            out[rows, cols] = (base[rows, cols].astype(jnp.float32) + tile).astype(jnp.bfloat16)


SMEM = pl.BlockSpec(memory_space=pltpu.SMEM)
VMEM = pl.BlockSpec(memory_space=pltpu.VMEM)
LIMIT = pltpu.CompilerParams(vmem_limit_bytes=32 * 1024 * 1024)


def tiles_call(kernel, n, name, specs, *args):
    return pl.pallas_call(
        kernel,
        out_shape=jax.ShapeDtypeStruct((n, BLK, BLK), jnp.bfloat16),
        in_specs=specs,
        out_specs=VMEM,
        compiler_params=LIMIT,
        name=name,
    )(*args)


def exchange(x, axes):
    return lax.all_to_all(x, axes, split_axis=0, concat_axis=0, tiled=True)


def shards(master_new, sent_base, rollout_base, tokens, lengths, expert_slot):
    sent = tiles_call(encode_kernel, 16, "encode", [SMEM, VMEM, VMEM], lengths, master_new, sent_base)
    home = exchange(sent, ("zl", "x", "c"))
    by_y = tiles_call(to_y_kernel, 8, "to_y", [SMEM, SMEM, VMEM], lengths, expert_slot, home)
    by_y = exchange(by_y, ("y",))
    by_z = tiles_call(to_z_kernel, 8, "to_z", [SMEM, VMEM], expert_slot, by_y)
    by_z = exchange(by_z, ("zh", "zl"))
    by_x = tiles_call(to_x_kernel, 24, "to_x", [VMEM], by_z)
    mine = exchange(by_x, ("x",))
    other = lax.ppermute(mine, "c", [(0, 1), (1, 0)])
    in_flight = lax.dot_general(
        tokens[0, 0], rollout_base, (((1,), (1,)), ((), ())), preferred_element_type=jnp.float32
    ).astype(jnp.bfloat16)[None, None]
    new_weights = pl.pallas_call(
        add_kernel,
        out_shape=jax.ShapeDtypeStruct(rollout_base.shape, jnp.bfloat16),
        in_specs=[SMEM, VMEM, VMEM, VMEM],
        out_specs=VMEM,
        compiler_params=LIMIT,
        name="add",
    )(expert_slot, mine, other, rollout_base)
    return (new_weights, in_flight)


def solution(mesh):
    fine = Mesh(mesh.devices.reshape(2, 4, 2, 4, 8), ("zl", "x", "c", "zh", "y"))
    group, shard = ("zl", "x", "c"), ("zh", "y")
    placed = (
        P(shard, group, None, None),
        P(shard, group, None, None),
        P(shard, None),
        P(group, shard, None, None),
        P(),
        P(),
    )
    return jax.shard_map(
        shards,
        mesh=fine,
        in_specs=placed,
        out_specs=(P(shard, None), P(group, shard, None, None)),
        check_vma=False,
    )
```

```python
import jax
import jax.numpy as jnp
import numpy as np
from jax import lax
from jax.experimental import pallas as pl
from jax.experimental.pallas import tpu as pltpu
from jax.sharding import Mesh
from jax.sharding import PartitionSpec as P

CLIP_RATIO = 2.5
EPSILON = 1e-06

AXES = {"zl": 2, "x": 4, "c": 2, "zh": 4, "ya": 2, "yb": 2, "yc": 2}
BLK = 128
HALF = 64
TROWS = 12
MOST = 6
GROUPS = 16
EXPERTS = 8


class Place:
    def __init__(self):
        at = {name: lax.axis_index(name) for name in AXES}
        self.c, self.zh, self.ya, self.yc = at["c"], at["zh"], at["ya"], at["yc"]
        self.g = at["zl"] * 8 + at["x"] * 2 + at["c"]
        self.cc = at["zh"] * 4 + at["ya"] * 2 + at["yb"]
        self.own = at["zh"] * 4 + at["yb"] * 2 + at["yc"]


def run_of(lengths, s, g):
    start = jnp.int32(0)
    for i in range(GROUPS):
        start += jnp.where(i < g, lengths[i, s], 0)
    return start, lengths[g, s]


def encode_kernel(lengths, master, sent, keep, give):
    at = Place()
    start, count = run_of(lengths, 2 * at.cc + at.yc, at.g)
    for j in range(MOST):
        change = master[0, j] - sent[0, j].astype(jnp.float32)
        mean = jnp.sum(change * change, axis=(0, 1), keepdims=True) * (1.0 / (BLK * BLK))
        scale = jnp.sqrt(mean + EPSILON).astype(jnp.bfloat16).astype(jnp.float32)
        encoded = jnp.clip(change / scale, -CLIP_RATIO, CLIP_RATIO).astype(jnp.bfloat16)
        value = (encoded.astype(jnp.float32) * scale).astype(jnp.bfloat16)
        r = lax.rem(start + j, TROWS)
        here = lax.bitwise_and(lax.bitwise_xor(lax.div(r, 3), at.cc), 1) == at.c

        @pl.when((j < count) & here)
        def _():
            keep[lax.rem(r, 3)] = value

        @pl.when((j < count) & jnp.logical_not(here))
        def _():
            give[lax.rem(r, 3)] = value


def home_kernel(lengths, slots, keep, got, out):
    at = Place()
    for tiles, g in ((keep, at.g), (got, lax.bitwise_xor(at.g, 1))):
        start, count = run_of(lengths, 2 * at.cc + at.yc, g)
        for j in range(MOST):
            q = lax.min(start + j, 47)
            r = lax.rem(q, TROWS)
            k, i = lax.div(r, 3), lax.rem(r, 3)
            p = slots[4 * at.yc + lax.div(q, TROWS)]
            home = lax.bitwise_xor(4 * lax.div(p, 2) + k, at.cc)

            @pl.when((j < count) & (lax.bitwise_and(home, 1) == at.c))
            def _():
                peer = lax.bitwise_and(home, 14)
                out[peer, i] = tiles[i, :HALF, :]
                out[peer + 1, i] = tiles[i, HALF:, :]


def part_kernel(lengths, slots, got, first, second):
    at = Place()
    m = lax.bitwise_xor(at.g, at.cc)
    k = lax.bitwise_and(m, 3)
    for part, out in ((at.yc, first), (1 - at.yc, second)):
        p = 2 * lax.div(m, 4) + part
        e = jnp.int32(0)
        for n in range(EXPERTS):
            e += jnp.where(slots[n] == p, n, 0)
        side = lax.div(e, 4)
        q = lax.rem(e, 4) * TROWS + 3 * k
        owners = [jnp.int32(0)] * 3
        end = jnp.int32(0)
        for n in range(GROUPS - 1):
            end += lengths[n, 2 * at.cc + side]
            for i in range(3):
                owners[i] += jnp.where(end <= q + i, 1, 0)
        for i in range(3):
            out[i] = got[lax.bitwise_and(owners[i], 14) + side, i]


def spread_kernel(first, second, out):
    at = Place()
    near = pl.ds(pl.multiple_of(at.ya * HALF, HALF), HALF)
    far = pl.ds(pl.multiple_of((1 - at.ya) * HALF, HALF), HALF)
    for i in range(3):
        for to in range(8):
            out[to, i, near, :] = first[i]
            out[to, i, far, :] = second[i]


def add_kernel(mine, other, base, out):
    at = Place()
    for col in range(16):
        g = lax.bitwise_xor(at.own, col)
        near = lax.bitwise_and(g, 1) == at.c
        chip = lax.div(g, 2)
        for i in range(3):
            tile = jnp.where(near, mine[chip, i], other[chip, i]).astype(jnp.float32)
            rows, cols = pl.ds(i * BLK, BLK), pl.ds(col * BLK, BLK)
            out[rows, cols] = (base[rows, cols].astype(jnp.float32) + tile).astype(jnp.bfloat16)


SMEM = pl.BlockSpec(memory_space=pltpu.SMEM)
VMEM = pl.BlockSpec(memory_space=pltpu.VMEM)


def call(kernel, name, specs, shapes, *args):
    outs = tuple(jax.ShapeDtypeStruct(s, jnp.bfloat16) for s in shapes)
    return pl.pallas_call(
        kernel,
        out_shape=outs,
        in_specs=specs,
        out_specs=(VMEM,) * len(outs),
        compiler_params=pltpu.CompilerParams(vmem_limit_bytes=32 * 1024 * 1024),
        name=name,
    )(*args)


def exchange(x, axes):
    return lax.all_to_all(x, axes, split_axis=0, concat_axis=0, tiled=True)


def routes(flip):
    sizes = tuple(AXES.values())
    pairs = []
    for n in range(512):
        zl, x, c, zh, ya, yb, yc = (int(v) for v in np.unravel_index(n, sizes))
        m = (zl * 8 + x * 2 + c) ^ (zh * 4 + ya * 2 + yb)
        to = (zl, x, c, m // 4, yc ^ flip, (m // 2) % 2, m % 2)
        pairs.append((n, int(np.ravel_multi_index(to, sizes))))
    return pairs


def shards(master_new, sent_base, rollout_base, tokens, lengths, expert_slot):
    lengths = lengths.T
    keep, give = call(
        encode_kernel, "encode", [SMEM, VMEM, VMEM], [(3, BLK, BLK)] * 2, lengths, master_new, sent_base
    )
    got = lax.ppermute(give, "c", [(0, 1), (1, 0)])
    (out,) = call(
        home_kernel, "home", [SMEM, SMEM, VMEM, VMEM], [(16, 3, HALF, BLK)], lengths, expert_slot, keep, got
    )
    home = exchange(out, ("zl", "x", "yc"))
    first, second = call(
        part_kernel, "part", [SMEM, SMEM, VMEM], [(3, HALF, BLK)] * 2, lengths, expert_slot, home
    )
    first = lax.ppermute(first, tuple(AXES), routes(0))
    second = lax.ppermute(second, tuple(AXES), routes(1))
    (out,) = call(spread_kernel, "spread", [VMEM, VMEM], [(8, 3, BLK, BLK)], first, second)
    mine = exchange(out, ("zl", "x"))
    other = lax.ppermute(mine, "c", [(0, 1), (1, 0)])
    in_flight = lax.dot_general(
        tokens[0, 0], rollout_base, (((1,), (1,)), ((), ())), preferred_element_type=jnp.float32
    ).astype(jnp.bfloat16)[None, None]
    (new_weights,) = call(
        add_kernel, "add", [VMEM, VMEM, VMEM], [rollout_base.shape], mine, other, rollout_base
    )
    return (new_weights, in_flight)


def solution(mesh):
    fine = Mesh(mesh.devices.reshape(tuple(AXES.values())), tuple(AXES))
    group, shard = ("zl", "x", "c"), ("zh", "ya", "yb", "yc")
    placed = (
        P(shard, group, None, None),
        P(shard, group, None, None),
        P(shard, None),
        P(group, shard, None, None),
        P(),
        P(),
    )
    return jax.shard_map(
        shards,
        mesh=fine,
        in_specs=placed,
        out_specs=(P(shard, None), P(group, shard, None, None)),
        check_vma=False,
    )
```

```python
import jax
import jax.numpy as jnp
from jax import lax
from jax.experimental import pallas as pl
from jax.experimental.pallas import tpu as pltpu
from jax.sharding import Mesh
from jax.sharding import PartitionSpec as P

CLIP_RATIO = 2.5
EPSILON = 1e-06

AXES = {"zl": 2, "x": 4, "c": 2, "zh": 4, "ya": 2, "yb": 2, "yc": 2}
BLK = 128
HALF = 64
PART = 16
TROWS = 12
MOST = 6
GROUPS = 16
EXPERTS = 8


class Place:
    def __init__(self):
        at = {name: lax.axis_index(name) for name in AXES}
        self.c, self.x, self.yb, self.yc = at["c"], at["x"], at["yb"], at["yc"]
        self.g = at["zl"] * 8 + at["x"] * 2 + at["c"]
        self.col = at["zh"] * 4 + at["ya"] * 2 + at["yb"]
        self.s = 2 * self.col + at["yc"]


def run_of(lengths, s, g):
    start = jnp.int32(0)
    for i in range(GROUPS):
        start += jnp.where(i < g, lengths[i, s], 0)
    return start, lengths[g, s]


def encode_kernel(master, sent, keep, give):
    at = Place()
    change = master[0, 0] - sent[0, 0].astype(jnp.float32)
    mean = jnp.sum(change * change, axis=(0, 1), keepdims=True) * (1.0 / (BLK * BLK))
    scale = jnp.sqrt(mean + EPSILON).astype(jnp.bfloat16).astype(jnp.float32)
    encoded = jnp.clip(change / scale, -CLIP_RATIO, CLIP_RATIO).astype(jnp.bfloat16)
    value = (encoded.astype(jnp.float32) * scale).astype(jnp.bfloat16)
    low = at.c == 0
    keep[0] = jnp.where(low, value[:HALF], value[HALF:])
    give[0] = jnp.where(low, value[HALF:], value[:HALF])


def home_kernel(lengths, keep, got, out):
    at = Place()
    for tiles, g in ((keep, at.g), (got, at.g ^ 1)):
        start, count = run_of(lengths, at.s, g)
        for j in range(MOST):
            r = lax.rem(start + j, TROWS)
            k, i = lax.div(r, 3), lax.rem(r, 3)
            to = ((k >> 1) ^ at.yb) * 2 + (k & 1)

            @pl.when(j < count)
            def _():
                for n in range(4):
                    out[to + 4 * n, i] = tiles[j, n * PART : (n + 1) * PART, :]


def slot_kernel(lengths, slots, got, out):
    at = Place()
    kb = (at.x & 1) ^ at.yb
    first = 3 * (2 * kb + at.yc)
    ends = []
    for side in range(2):
        end, row = jnp.int32(0), []
        for n in range(GROUPS - 1):
            end += lengths[n, 2 * at.col + side]
            row.append(end)
        ends.append(row)
    for e in range(EXPERTS):
        to = 2 * slots[e] + kb
        for i in range(3):
            q = (e % 4) * TROWS + first + i
            owner = jnp.int32(0)
            for end in ends[e // 4]:
                owner += jnp.where(end <= q, 1, 0)
            out[to, i] = got[(owner & 14) + e // 4, i]


def spread_kernel(got, out):
    at = Place()
    side = (at.x & 1) ^ at.yb
    for n in range(8):
        for i in range(3):
            part = got[2 * n + side, i]
            for to in range(8):
                out[to, n, i] = part


def add_kernel(mine, other, base, out):
    at = Place()
    near = at.c == 0
    for col in range(16):
        cols = pl.ds(col * BLK, BLK)
        side = (col & 1) ^ at.yb
        for n in range(4):
            chip = 2 * n + side
            for i in range(3):
                a, b = mine[chip, col >> 1, i], other[chip, col >> 1, i]
                for half in range(2):
                    part = (jnp.where(near, b, a) if half else jnp.where(near, a, b)).astype(jnp.float32)
                    rows = pl.ds(i * BLK + half * HALF + n * PART, PART)
                    out[rows, cols] = (base[rows, cols].astype(jnp.float32) + part).astype(jnp.bfloat16)


SMEM = pl.BlockSpec(memory_space=pltpu.SMEM)
VMEM = pl.BlockSpec(memory_space=pltpu.VMEM)
LIMIT = pltpu.CompilerParams(vmem_limit_bytes=32 * 1024 * 1024)


def call(kernel, name, specs, shapes, *args):
    outs = tuple(jax.ShapeDtypeStruct(s, jnp.bfloat16) for s in shapes)
    return pl.pallas_call(
        kernel,
        out_shape=outs,
        in_specs=specs,
        out_specs=(VMEM,) * len(outs),
        compiler_params=LIMIT,
        name=name,
    )(*args)


def exchange(x, axes):
    return lax.all_to_all(x, axes, split_axis=0, concat_axis=0, tiled=True)


def shards(master_new, sent_base, rollout_base, tokens, lengths, expert_slot):
    lengths = lengths.T
    halves = jax.ShapeDtypeStruct((MOST, HALF, BLK), jnp.bfloat16)
    keep, give = pl.pallas_call(
        encode_kernel,
        grid=(MOST,),
        out_shape=(halves, halves),
        in_specs=[pl.BlockSpec((1, 1, BLK, BLK), lambda j: (0, j, 0, 0))] * 2,
        out_specs=(pl.BlockSpec((1, HALF, BLK), lambda j: (j, 0, 0)),) * 2,
        compiler_params=LIMIT,
        name="encode",
    )(master_new, sent_base)
    got = lax.ppermute(give, "c", [(0, 1), (1, 0)])
    (out,) = call(home_kernel, "home", [SMEM, VMEM, VMEM], [(16, 3, PART, BLK)], lengths, keep, got)
    out = exchange(out, ("zl", "x", "yc"))
    (out,) = call(slot_kernel, "slot", [SMEM, SMEM, VMEM], [(16, 3, PART, BLK)], lengths, expert_slot, out)
    out = exchange(out, ("zh", "ya", "yb"))
    (out,) = call(spread_kernel, "spread", [VMEM], [(8, 8, 3, PART, BLK)], out)
    mine = exchange(out, ("zl", "x"))
    other = lax.ppermute(mine, "c", [(0, 1), (1, 0)])
    in_flight = lax.dot_general(
        tokens[0, 0], rollout_base, (((1,), (1,)), ((), ())), preferred_element_type=jnp.float32
    ).astype(jnp.bfloat16)[None, None]
    (new_weights,) = call(
        add_kernel, "add", [VMEM, VMEM, VMEM], [rollout_base.shape], mine, other, rollout_base
    )
    return (new_weights, in_flight)


def solution(mesh):
    fine = Mesh(mesh.devices.reshape(tuple(AXES.values())), tuple(AXES))
    group, shard = ("zl", "x", "c"), ("zh", "ya", "yb", "yc")
    placed = (
        P(shard, group, None, None),
        P(shard, group, None, None),
        P(shard, None),
        P(group, shard, None, None),
        P(),
        P(),
    )
    return jax.shard_map(
        shards,
        mesh=fine,
        in_specs=placed,
        out_specs=(P(shard, None), P(group, shard, None, None)),
        check_vma=False,
    )
```

```python
import jax
import jax.numpy as jnp
from jax import lax
from jax.experimental import pallas as pl
from jax.experimental.pallas import tpu as pltpu
from jax.sharding import Mesh
from jax.sharding import PartitionSpec as P

CLIP_RATIO = 2.5
EPSILON = 1e-06

AXES = {"zl": 2, "x": 4, "c": 2, "zh": 4, "ya": 2, "yb": 2, "yc": 2}
BLK = 128
HALF = 64
PART = 16
TROWS = 12
MOST = 6
GROUPS = 16
EXPERTS = 8


class Place:
    def __init__(self):
        at = {name: lax.axis_index(name) for name in AXES}
        self.c, self.x, self.yb, self.yc = at["c"], at["x"], at["yb"], at["yc"]
        self.g = at["zl"] * 8 + at["x"] * 2 + at["c"]
        self.col = at["zh"] * 4 + at["ya"] * 2 + at["yb"]
        self.s = 2 * self.col + at["yc"]


def run_of(lengths, s, g):
    start = jnp.int32(0)
    for i in range(GROUPS):
        start += jnp.where(i < g, lengths[i, s], 0)
    return start, lengths[g, s]


def encode_kernel(lengths_in, slots_in, master_in, sent_in, out, lengths_out, slots_out, lengths, master, sent, sems):
    loads = [
        pltpu.make_async_copy(lengths_in, lengths, sems.at[0]),
        pltpu.make_async_copy(lengths_in, lengths_out, sems.at[1]),
        pltpu.make_async_copy(slots_in, slots_out, sems.at[2]),
    ]
    for j in range(MOST):
        loads.append(pltpu.make_async_copy(master_in.at[0, j], master.at[j], sems.at[3 + 2 * j]))
        loads.append(pltpu.make_async_copy(sent_in.at[0, j], sent.at[j], sems.at[4 + 2 * j]))
    for load in loads:
        load.start()
    at = Place()
    loads[0].wait()
    start, count = run_of(lengths, at.s, at.g)
    for j in range(MOST):
        loads[3 + 2 * j].wait()
        loads[4 + 2 * j].wait()
        change = master[j] - sent[j].astype(jnp.float32)
        mean = jnp.sum(change * change, axis=(0, 1), keepdims=True) * (1.0 / (BLK * BLK))
        scale = jnp.sqrt(mean + EPSILON).astype(jnp.bfloat16).astype(jnp.float32)
        encoded = jnp.clip(change / scale, -CLIP_RATIO, CLIP_RATIO).astype(jnp.bfloat16)
        value = (encoded.astype(jnp.float32) * scale).astype(jnp.bfloat16)
        r = lax.rem(start + j, TROWS)
        k, i = lax.div(r, 3), lax.rem(r, 3)
        to = ((k >> 1) ^ at.yb) * 4 + (k & 1)

        @pl.when(j < count)
        def _():
            for n in range(8):
                peer = (n >> 1 & 1) * 16 + (n & 1) * 8 + (n >> 2) * 2
                out[peer + to, i] = value[n * PART : (n + 1) * PART, :]

    loads[1].wait()
    loads[2].wait()


def slot_kernel(lengths, slots, got, out):
    at = Place()
    kb = (at.x & 1) ^ at.yb
    first = 3 * (2 * kb + at.yc)
    ends = []
    for side in range(2):
        end, row = jnp.int32(0), []
        for n in range(GROUPS - 1):
            end += lengths[n, 2 * at.col + side]
            row.append(end)
        ends.append(row)
    for e in range(EXPERTS):
        to = 2 * slots[e] + kb
        for i in range(3):
            q = (e % 4) * TROWS + first + i
            owner = jnp.int32(0)
            for end in ends[e // 4]:
                owner += jnp.where(end <= q, 1, 0)
            out[to, i] = got[2 * owner + e // 4, i]


def spread_kernel(got, out):
    at = Place()
    side = (at.x & 1) ^ at.yb
    for n in range(8):
        for i in range(3):
            part = got[2 * n + side, i]
            for to in range(8):
                out[to, n, i] = part


def add_kernel(mine, other, base, out):
    at = Place()
    near = at.c == 0
    for col in range(16):
        cols = pl.ds(col * BLK, BLK)
        side = (col & 1) ^ at.yb
        for n in range(4):
            chip = 2 * n + side
            for i in range(3):
                a, b = mine[chip, col >> 1, i], other[chip, col >> 1, i]
                for half in range(2):
                    part = (jnp.where(near, b, a) if half else jnp.where(near, a, b)).astype(jnp.float32)
                    rows = pl.ds(i * BLK + half * HALF + n * PART, PART)
                    out[rows, cols] = (base[rows, cols].astype(jnp.float32) + part).astype(jnp.bfloat16)


SMEM = pl.BlockSpec(memory_space=pltpu.SMEM)
VMEM = pl.BlockSpec(memory_space=pltpu.VMEM)
HBM = pl.BlockSpec(memory_space=pltpu.HBM)
LIMIT = pltpu.CompilerParams(vmem_limit_bytes=32 * 1024 * 1024)


def call(kernel, name, specs, shapes, *args):
    outs = tuple(jax.ShapeDtypeStruct(s, jnp.bfloat16) for s in shapes)
    return pl.pallas_call(
        kernel,
        out_shape=outs,
        in_specs=specs,
        out_specs=(VMEM,) * len(outs),
        compiler_params=LIMIT,
        name=name,
    )(*args)


def exchange(x, axes):
    return lax.all_to_all(x, axes, split_axis=0, concat_axis=0, tiled=True)


def shards(master_new, sent_base, rollout_base, tokens, lengths, expert_slot):
    lengths = lengths.T
    out, lengths, expert_slot = pl.pallas_call(
        encode_kernel,
        out_shape=(
            jax.ShapeDtypeStruct((32, 3, PART, BLK), jnp.bfloat16),
            jax.typeof(lengths),
            jax.typeof(expert_slot),
        ),
        in_specs=[HBM] * 4,
        out_specs=(VMEM,) * 3,
        scratch_shapes=[
            pltpu.SMEM(lengths.shape, jnp.int32),
            pltpu.VMEM((MOST, BLK, BLK), jnp.float32),
            pltpu.VMEM((MOST, BLK, BLK), jnp.bfloat16),
            pltpu.SemaphoreType.DMA((3 + 2 * MOST,)),
        ],
        compiler_params=LIMIT,
        name="encode",
    )(*(pltpu.with_memory_space_constraint(v, pltpu.HBM) for v in (lengths, expert_slot, master_new, sent_base)))
    out = exchange(out, ("zl", "x", "c", "yc"))
    (out,) = call(slot_kernel, "slot", [SMEM, SMEM, VMEM], [(16, 3, PART, BLK)], lengths, expert_slot, out)
    out = exchange(out, ("zh", "ya", "yb"))
    (out,) = call(spread_kernel, "spread", [VMEM], [(8, 8, 3, PART, BLK)], out)
    mine = exchange(out, ("zl", "x"))
    other = lax.ppermute(mine, "c", [(0, 1), (1, 0)])
    in_flight = lax.dot_general(
        tokens[0, 0], rollout_base, (((1,), (1,)), ((), ())), preferred_element_type=jnp.float32
    ).astype(jnp.bfloat16)[None, None]
    (new_weights,) = call(
        add_kernel, "add", [VMEM, VMEM, VMEM], [rollout_base.shape], mine, other, rollout_base
    )
    return (new_weights, in_flight)


def solution(mesh):
    fine = Mesh(mesh.devices.reshape(tuple(AXES.values())), tuple(AXES))
    group, shard = ("zl", "x", "c"), ("zh", "ya", "yb", "yc")
    placed = (
        P(shard, group, None, None),
        P(shard, group, None, None),
        P(shard, None),
        P(group, shard, None, None),
        P(),
        P(),
    )
    return jax.shard_map(
        shards,
        mesh=fine,
        in_specs=placed,
        out_specs=(P(shard, None), P(group, shard, None, None)),
        check_vma=False,
    )
```

```python
import jax
import jax.numpy as jnp
from jax import lax
from jax.experimental import pallas as pl
from jax.experimental.pallas import tpu as pltpu
from jax.sharding import Mesh
from jax.sharding import PartitionSpec as P

CLIP_RATIO = 2.5
EPSILON = 1e-06

AXES = {"zl": 2, "x": 4, "c": 2, "zh": 4, "ya": 2, "yb": 2, "yc": 2}
BLK = 128
HALF = 64
PART = 16
TROWS = 12
MOST = 6
GROUPS = 16
EXPERTS = 8


class Place:
    def __init__(self):
        at = {name: lax.axis_index(name) for name in AXES}
        self.c, self.x, self.yb, self.yc = at["c"], at["x"], at["yb"], at["yc"]
        self.g = at["zl"] * 8 + at["x"] * 2 + at["c"]
        self.col = at["zh"] * 4 + at["ya"] * 2 + at["yb"]
        self.s = 2 * self.col + at["yc"]


def encode_kernel(lengths_in, slots_in, master_in, sent_in, out, lengths_out, slots_out, lengths, master, sent, sems):
    loads = [
        pltpu.make_async_copy(lengths_in, lengths, sems.at[0]),
        pltpu.make_async_copy(lengths_in, lengths_out, sems.at[1]),
        pltpu.make_async_copy(slots_in, slots_out, sems.at[2]),
    ]
    for j in range(MOST):
        loads.append(pltpu.make_async_copy(master_in.at[0, j], master.at[j], sems.at[3 + 2 * j]))
        loads.append(pltpu.make_async_copy(sent_in.at[0, j], sent.at[j], sems.at[4 + 2 * j]))
    for load in loads:
        load.start()
    at = Place()
    loads[0].wait()
    start = jnp.int32(0)
    for n in range(GROUPS - 1):
        start += jnp.where(n < at.g, lengths[n, at.s], 0)
    for load in loads[3:]:
        load.wait()
    for j in range(MOST):
        change = master[j] - sent[j].astype(jnp.float32)
        mean = jnp.sum(change * change, axis=(0, 1), keepdims=True) * (1.0 / (BLK * BLK))
        scale = jnp.sqrt(mean + EPSILON).astype(jnp.bfloat16).astype(jnp.float32)
        encoded = jnp.clip(change / scale, -CLIP_RATIO, CLIP_RATIO).astype(jnp.bfloat16)
        value = (encoded.astype(jnp.float32) * scale).astype(jnp.bfloat16)
        r = lax.rem(start + j, TROWS)
        k, i = lax.div(r, 3), lax.rem(r, 3)
        to = ((k >> 1) ^ at.yb) * 4 + (k & 1)
        for n in range(8):
            peer = (n >> 1 & 1) * 16 + (n & 1) * 8 + (n >> 2) * 2
            out[peer + to, i] = value[n * PART : (n + 1) * PART, :]

    loads[1].wait()
    loads[2].wait()


def slot_kernel(lengths, slots, got, out):
    at = Place()
    kb = (at.x & 1) ^ at.yb
    first = 3 * (2 * kb + at.yc)
    ends = []
    for side in range(2):
        end, row = jnp.int32(0), []
        for n in range(GROUPS - 1):
            end += lengths[n, 2 * at.col + side]
            row.append(end)
        ends.append(row)
    for e in range(EXPERTS):
        to = 2 * slots[e] + kb
        for i in range(3):
            q = (e % 4) * TROWS + first + i
            owner = jnp.int32(0)
            for end in ends[e // 4]:
                owner += jnp.where(end <= q, 1, 0)
            out[to, i] = got[2 * owner + e // 4, i]


def spread_kernel(got, out):
    at = Place()
    side = (at.x & 1) ^ at.yb
    for n in range(8):
        for i in range(3):
            part = got[2 * n + side, i]
            for to in range(8):
                out[to, n, i] = part


def add_half(half, tiles, base, out, done, sems):
    at = Place()
    stores = []
    for i in range(3):
        first = pl.multiple_of(i * BLK + half(at.c) * HALF, HALF)
        for n in range(4):
            rows = pl.ds(pl.multiple_of(first + n * PART, PART), PART)
            for col in range(16):
                cols = pl.ds(col * BLK, BLK)
                part = tiles[2 * n + ((col & 1) ^ at.yb), col >> 1, i].astype(jnp.float32)
                done[i, n * PART : (n + 1) * PART, cols] = (base[rows, cols].astype(jnp.float32) + part).astype(jnp.bfloat16)
        stores.append(pltpu.make_async_copy(done.at[i], out.at[pl.ds(first, HALF)], sems.at[i]))
        stores[i].start()
    for store in stores:
        store.wait()


def add_mine_kernel(mine, base, out, done, sems):
    add_half(lambda c: c, mine, base, out, done, sems)


def add_other_kernel(other, base, begun, out, done, sems):
    add_half(lambda c: 1 - c, other, base, out, done, sems)


SMEM = pl.BlockSpec(memory_space=pltpu.SMEM)
VMEM = pl.BlockSpec(memory_space=pltpu.VMEM)
HBM = pl.BlockSpec(memory_space=pltpu.HBM)
LIMIT = pltpu.CompilerParams(vmem_limit_bytes=32 * 1024 * 1024)


def call(kernel, name, specs, shapes, *args):
    outs = tuple(jax.ShapeDtypeStruct(s, jnp.bfloat16) for s in shapes)
    return pl.pallas_call(
        kernel,
        out_shape=outs,
        in_specs=specs,
        out_specs=(VMEM,) * len(outs),
        compiler_params=LIMIT,
        name=name,
    )(*args)


def add_call(kernel, name, tiles, base, *begun):
    return pl.pallas_call(
        kernel,
        out_shape=jax.typeof(base),
        in_specs=[VMEM, VMEM] + [HBM] * len(begun),
        out_specs=HBM,
        scratch_shapes=[pltpu.VMEM((3, HALF, base.shape[1]), jnp.bfloat16), pltpu.SemaphoreType.DMA((3,))],
        input_output_aliases={2: 0} if begun else {},
        compiler_params=LIMIT,
        name=name,
    )(tiles, base, *begun)


def exchange(x, axes):
    return lax.all_to_all(x, axes, split_axis=0, concat_axis=0, tiled=True)


def shards(master_new, sent_base, rollout_base, tokens, lengths, expert_slot):
    lengths = lengths.T
    out, lengths, expert_slot = pl.pallas_call(
        encode_kernel,
        out_shape=(
            jax.ShapeDtypeStruct((32, 3, PART, BLK), jnp.bfloat16),
            jax.typeof(lengths),
            jax.typeof(expert_slot),
        ),
        in_specs=[HBM] * 4,
        out_specs=(VMEM,) * 3,
        scratch_shapes=[
            pltpu.SMEM(lengths.shape, jnp.int32),
            pltpu.VMEM((MOST, BLK, BLK), jnp.float32),
            pltpu.VMEM((MOST, BLK, BLK), jnp.bfloat16),
            pltpu.SemaphoreType.DMA((3 + 2 * MOST,)),
        ],
        compiler_params=LIMIT,
        name="encode",
    )(*(pltpu.with_memory_space_constraint(v, pltpu.HBM) for v in (lengths, expert_slot, master_new, sent_base)))
    out = exchange(out, ("zl", "x", "c", "yc"))
    (out,) = call(slot_kernel, "slot", [SMEM, SMEM, VMEM], [(16, 3, PART, BLK)], lengths, expert_slot, out)
    out = exchange(out, ("zh", "ya", "yb"))
    (out,) = call(spread_kernel, "spread", [VMEM], [(8, 8, 3, PART, BLK)], out)
    mine = exchange(out, ("zl", "x"))
    other = lax.ppermute(mine, "c", [(0, 1), (1, 0)])
    in_flight = lax.dot_general(
        tokens[0, 0], rollout_base, (((1,), (1,)), ((), ())), preferred_element_type=jnp.float32
    ).astype(jnp.bfloat16)[None, None]
    begun = add_call(add_mine_kernel, "add_mine", mine, rollout_base)
    new_weights = add_call(add_other_kernel, "add_other", other, rollout_base, begun)
    return (new_weights, in_flight)


def solution(mesh):
    fine = Mesh(mesh.devices.reshape(tuple(AXES.values())), tuple(AXES))
    group, shard = ("zl", "x", "c"), ("zh", "ya", "yb", "yc")
    placed = (
        P(shard, group, None, None),
        P(shard, group, None, None),
        P(shard, None),
        P(group, shard, None, None),
        P(),
        P(),
    )
    return jax.shard_map(
        shards,
        mesh=fine,
        in_specs=placed,
        out_specs=(P(shard, None), P(group, shard, None, None)),
        check_vma=False,
    )
```

```python
import jax
import jax.numpy as jnp
from jax import lax
from jax.experimental import pallas as pl
from jax.experimental.pallas import tpu as pltpu
from jax.sharding import Mesh
from jax.sharding import PartitionSpec as P

CLIP_RATIO = 2.5
EPSILON = 1e-06

AXES = {"zl": 2, "x": 4, "c": 2, "zh": 4, "ya": 2, "yb": 2, "yc": 2}
BLK = 128
HALF = 64
PART = 16
TROWS = 12
MOST = 6
GROUPS = 16
EXPERTS = 8


class Place:
    def __init__(self):
        at = {name: lax.axis_index(name) for name in AXES}
        self.c, self.x, self.yb, self.yc = at["c"], at["x"], at["yb"], at["yc"]
        self.g = at["zl"] * 8 + at["x"] * 2 + at["c"]
        self.col = at["zh"] * 4 + at["ya"] * 2 + at["yb"]
        self.s = 2 * self.col + at["yc"]


def encode_kernel(lengths_in, slots_in, master_in, sent_in, out, lengths_out, slots_out, lengths, master, sent, sems):
    loads = [
        pltpu.make_async_copy(lengths_in, lengths, sems.at[0]),
        pltpu.make_async_copy(lengths_in, lengths_out, sems.at[1]),
        pltpu.make_async_copy(slots_in, slots_out, sems.at[2]),
    ]
    for j in range(MOST):
        loads.append(pltpu.make_async_copy(master_in.at[0, j], master.at[j], sems.at[3 + 2 * j]))
        loads.append(pltpu.make_async_copy(sent_in.at[0, j], sent.at[j], sems.at[4 + 2 * j]))
    for load in loads:
        load.start()
    at = Place()
    loads[0].wait()
    start = jnp.int32(0)
    for n in range(GROUPS - 1):
        start += jnp.where(n < at.g, lengths[n, at.s], 0)
    for load in loads[3:]:
        load.wait()
    for j in range(MOST):
        change = master[j] - sent[j].astype(jnp.float32)
        mean = jnp.sum(change * change, axis=(0, 1), keepdims=True) * (1.0 / (BLK * BLK))
        scale = jnp.sqrt(mean + EPSILON).astype(jnp.bfloat16).astype(jnp.float32)
        encoded = jnp.clip(change / scale, -CLIP_RATIO, CLIP_RATIO).astype(jnp.bfloat16)
        value = (encoded.astype(jnp.float32) * scale).astype(jnp.bfloat16)
        r = lax.rem(start + j, TROWS)
        k, i = lax.div(r, 3), lax.rem(r, 3)
        to = (((k >> 1) + i + at.yb) & 1) * 4 + (k & 1)
        slot = 0 if j < 2 else 1 if j == 5 else i >> 1
        for n in range(8):
            peer = (n >> 1 & 1) * 16 + (n & 1) * 8 + (n >> 2) * 2
            out[peer + to, slot] = value[n * PART : (n + 1) * PART, :]

    loads[1].wait()
    loads[2].wait()


def slot_kernel(lengths, slots, got, out, table):
    at = Place()
    for side in range(2):
        start = jnp.int32(0)
        for n in range(GROUPS):
            for j in range(MOST):
                table[side, start + j] = n * 8 + j
            start += lengths[n, 2 * at.col + side]
    odd = (at.x + at.yb) & 1
    for e in range(EXPERTS):
        p = slots[e]
        for i in range(3):
            kb = odd ^ (i & 1)
            entry = table[e // 4, (e % 4) * TROWS + 6 * kb + 3 * at.yc + i]
            slot = jnp.where((entry & 7) >= (2 if i == 2 else 5), 1, 0)
            out[2 * p + kb, i >> 1] = got[(entry >> 3) * 2 + e // 4, slot]


def spread_kernel(got, out):
    at = Place()
    side = (at.x + at.yb) & 1
    for n in range(8):
        parts = (got[2 * n + side, 0], got[2 * n + side, 1], got[2 * n + 1 - side, 0])
        for to in range(8):
            for m in range(3):
                out[to, n, m] = parts[m]


def add_half(half, tiles, base, out, done, sems):
    at = Place()
    stores = []
    for i in range(3):
        first = pl.multiple_of(i * BLK + half(at.c) * HALF, HALF)
        for n in range(4):
            rows = pl.ds(pl.multiple_of(first + n * PART, PART), PART)
            for col in range(16):
                cols = pl.ds(col * BLK, BLK)
                part = tiles[2 * n + ((at.yb + i + col) & 1), col >> 1, (0, 2, 1)[i]].astype(jnp.float32)
                done[i, n * PART : (n + 1) * PART, cols] = (base[rows, cols].astype(jnp.float32) + part).astype(jnp.bfloat16)
        stores.append(pltpu.make_async_copy(done.at[i], out.at[pl.ds(first, HALF)], sems.at[i]))
        stores[i].start()
    for store in stores:
        store.wait()


def add_mine_kernel(mine, base, out, done, sems):
    add_half(lambda c: c, mine, base, out, done, sems)


def add_other_kernel(other, base, begun, out, done, sems):
    add_half(lambda c: 1 - c, other, base, out, done, sems)


SMEM = pl.BlockSpec(memory_space=pltpu.SMEM)
VMEM = pl.BlockSpec(memory_space=pltpu.VMEM)
HBM = pl.BlockSpec(memory_space=pltpu.HBM)
LIMIT = pltpu.CompilerParams(vmem_limit_bytes=32 * 1024 * 1024)


def call(kernel, name, specs, shapes, *args, scratch=()):
    outs = tuple(jax.ShapeDtypeStruct(s, jnp.bfloat16) for s in shapes)
    return pl.pallas_call(
        kernel,
        out_shape=outs,
        in_specs=specs,
        out_specs=(VMEM,) * len(outs),
        scratch_shapes=scratch,
        compiler_params=LIMIT,
        name=name,
    )(*args)


def add_call(kernel, name, tiles, base, *begun):
    return pl.pallas_call(
        kernel,
        out_shape=jax.typeof(base),
        in_specs=[VMEM, VMEM] + [HBM] * len(begun),
        out_specs=HBM,
        scratch_shapes=[pltpu.VMEM((3, HALF, base.shape[1]), jnp.bfloat16), pltpu.SemaphoreType.DMA((3,))],
        input_output_aliases={2: 0} if begun else {},
        compiler_params=LIMIT,
        name=name,
    )(tiles, base, *begun)


def exchange(x, axes):
    return lax.all_to_all(x, axes, split_axis=0, concat_axis=0, tiled=True)


def shards(master_new, sent_base, rollout_base, tokens, lengths, expert_slot):
    lengths = lengths.T
    out, lengths, expert_slot = pl.pallas_call(
        encode_kernel,
        out_shape=(
            jax.ShapeDtypeStruct((32, 2, PART, BLK), jnp.bfloat16),
            jax.typeof(lengths),
            jax.typeof(expert_slot),
        ),
        in_specs=[HBM] * 4,
        out_specs=(VMEM,) * 3,
        scratch_shapes=[
            pltpu.SMEM(lengths.shape, jnp.int32),
            pltpu.VMEM((MOST, BLK, BLK), jnp.float32),
            pltpu.VMEM((MOST, BLK, BLK), jnp.bfloat16),
            pltpu.SemaphoreType.DMA((3 + 2 * MOST,)),
        ],
        compiler_params=LIMIT,
        name="encode",
    )(*(pltpu.with_memory_space_constraint(v, pltpu.HBM) for v in (lengths, expert_slot, master_new, sent_base)))
    out = exchange(out, ("zl", "x", "c", "yc"))
    (out,) = call(
        slot_kernel, "slot", [SMEM, SMEM, VMEM], [(16, 2, PART, BLK)], lengths, expert_slot, out,
        scratch=[pltpu.SMEM((2, 64), jnp.int32)],
    )
    out = exchange(out, ("zh", "ya", "yb"))
    (out,) = call(spread_kernel, "spread", [VMEM], [(8, 8, 3, PART, BLK)], out)
    mine = exchange(out, ("zl", "x"))
    other = lax.ppermute(mine, "c", [(0, 1), (1, 0)])
    in_flight = lax.dot_general(
        tokens[0, 0], rollout_base, (((1,), (1,)), ((), ())), preferred_element_type=jnp.float32
    ).astype(jnp.bfloat16)[None, None]
    begun = add_call(add_mine_kernel, "add_mine", mine, rollout_base)
    new_weights = add_call(add_other_kernel, "add_other", other, rollout_base, begun)
    return (new_weights, in_flight)


def solution(mesh):
    fine = Mesh(mesh.devices.reshape(tuple(AXES.values())), tuple(AXES))
    group, shard = ("zl", "x", "c"), ("zh", "ya", "yb", "yc")
    placed = (
        P(shard, group, None, None),
        P(shard, group, None, None),
        P(shard, None),
        P(group, shard, None, None),
        P(),
        P(),
    )
    return jax.shard_map(
        shards,
        mesh=fine,
        in_specs=placed,
        out_specs=(P(shard, None), P(group, shard, None, None)),
        check_vma=False,
    )
```

```python
import jax
import jax.numpy as jnp
import numpy as np
from jax import lax
from jax.experimental import pallas as pl
from jax.experimental.pallas import tpu as pltpu
from jax.sharding import Mesh
from jax.sharding import PartitionSpec as P

CLIP_RATIO = 2.5
EPSILON = 1e-06

AXES = {"zl": 2, "x": 4, "c": 2, "zh": 4, "ya": 2, "yb": 2, "yc": 2}
BLK = 128
HALF = 64
PART = 16
TROWS = 12
MOST = 6
GROUPS = 16
EXPERTS = 8


class Place:
    def __init__(self):
        at = {name: lax.axis_index(name) for name in AXES}
        self.c, self.x, self.yb, self.yc = at["c"], at["x"], at["yb"], at["yc"]
        self.g = at["zl"] * 8 + at["x"] * 2 + at["c"]
        self.turn = (at["zh"] >> 1) ^ (at["zh"] & 1)
        self.col = at["zh"] * 4 + at["ya"] * 2 + at["yb"]
        self.s = 2 * self.col + at["yc"]


def encode_kernel(lengths_in, slots_in, master_in, sent_in, out, lengths_out, slots_out, lengths, master, sent, sems):
    loads = [
        pltpu.make_async_copy(lengths_in, lengths, sems.at[0]),
        pltpu.make_async_copy(lengths_in, lengths_out, sems.at[1]),
        pltpu.make_async_copy(slots_in, slots_out, sems.at[2]),
    ]
    for j in range(MOST):
        loads.append(pltpu.make_async_copy(master_in.at[0, j], master.at[j], sems.at[3 + 2 * j]))
        loads.append(pltpu.make_async_copy(sent_in.at[0, j], sent.at[j], sems.at[4 + 2 * j]))
    for load in loads:
        load.start()
    at = Place()
    loads[0].wait()
    start = jnp.int32(0)
    for n in range(GROUPS - 1):
        start += jnp.where(n < at.g, lengths[n, at.s], 0)
    for load in loads[3:]:
        load.wait()
    for j in range(MOST):
        change = master[j] - sent[j].astype(jnp.float32)
        mean = jnp.sum(change * change, axis=(0, 1), keepdims=True) * (1.0 / (BLK * BLK))
        scale = jnp.sqrt(mean + EPSILON).astype(jnp.bfloat16).astype(jnp.float32)
        encoded = jnp.clip(change / scale, -CLIP_RATIO, CLIP_RATIO).astype(jnp.bfloat16)
        value = (encoded.astype(jnp.float32) * scale).astype(jnp.bfloat16)
        r = lax.rem(start + j, TROWS)
        k, i = lax.div(r, 3), lax.rem(r, 3)
        to = (((k >> 1) + i + at.yb) & 1) * 4 + (k & 1)
        slot = 0 if j < 2 else 1 if j == 5 else i >> 1
        for n in range(8):
            peer = ((n >> 1 & 1) ^ at.turn) * 16 + (n & 1) * 8 + (n >> 2) * 2
            out[peer + to, slot] = value[n * PART : (n + 1) * PART, :]

    loads[1].wait()
    loads[2].wait()


def slot_kernel(lengths, slots, got, out, table):
    at = Place()
    for side in range(2):
        start = jnp.int32(0)
        for n in range(GROUPS):
            for j in range(MOST):
                table[side, start + j] = n * 8 + j
            start += lengths[n, 2 * at.col + side]
    odd = (at.x + at.yb) & 1
    for e in range(EXPERTS):
        p = slots[e]
        for i in range(3):
            kb = odd ^ (i & 1)
            entry = table[e // 4, (e % 4) * TROWS + 6 * kb + 3 * at.yc + i]
            slot = jnp.where((entry & 7) >= (2 if i == 2 else 5), 1, 0)
            out[2 * p + kb, i >> 1] = got[(entry >> 3) * 2 + e // 4, slot]


def spread_kernel(got, out):
    at = Place()
    side = (at.x + at.yb) & 1
    for n in range(8):
        parts = (got[2 * n + side, 0], got[2 * n + side, 1], got[2 * n + 1 - side, 0])
        for to in range(8):
            for m in range(3):
                out[to, n, m] = parts[m]


def add_rows(at, half, i, tiles, base, new):
    for n in range(4):
        rows = pl.ds(pl.multiple_of(i * BLK + half * HALF + n * PART, PART), PART)
        for col in range(16):
            cols = pl.ds(col * BLK, BLK)
            chip = 4 * ((n >> 1) ^ at.turn) + 2 * (n & 1) + ((at.yb + i + col) & 1)
            part = tiles[chip, col >> 1, (0, 2, 1)[i]].astype(jnp.float32)
            new[i, n * PART : (n + 1) * PART, cols] = (base[rows, cols].astype(jnp.float32) + part).astype(jnp.bfloat16)


def add_mine_kernel(mine, base, new):
    at = Place()
    for i in range(3):
        add_rows(at, at.c, i, mine, base, new)


def add_other_kernel(other, base, new_mine, out, new, sems):
    at = Place()
    stores = []

    def store(half, i, rows):
        first = pl.multiple_of(i * BLK + half * HALF, HALF)
        stores.append(pltpu.make_async_copy(rows.at[i], out.at[pl.ds(first, HALF)], sems.at[len(stores)]))
        stores[-1].start()

    for i in range(3):
        store(at.c, i, new_mine)
    for i in range(3):
        add_rows(at, 1 - at.c, i, other, base, new)
        store(1 - at.c, i, new)
    for started in stores:
        started.wait()


SMEM = pl.BlockSpec(memory_space=pltpu.SMEM)
VMEM = pl.BlockSpec(memory_space=pltpu.VMEM)
HBM = pl.BlockSpec(memory_space=pltpu.HBM)
LIMIT = pltpu.CompilerParams(vmem_limit_bytes=32 * 1024 * 1024)


def call(kernel, name, specs, shapes, *args, scratch=()):
    outs = tuple(jax.ShapeDtypeStruct(s, jnp.bfloat16) for s in shapes)
    return pl.pallas_call(
        kernel,
        out_shape=outs,
        in_specs=specs,
        out_specs=(VMEM,) * len(outs),
        scratch_shapes=scratch,
        compiler_params=LIMIT,
        name=name,
    )(*args)


def exchange(x, axes):
    return lax.all_to_all(x, axes, split_axis=0, concat_axis=0, tiled=True)


def turned_groups():
    sizes = tuple(AXES.values())
    groups = []
    for side, x, c, yc in np.ndindex(2, 4, 2, 2):
        members = [(side ^ (zh >> 1) ^ (zh & 1), x, c, zh, ya, yb, yc) for zh, ya, yb in np.ndindex(4, 2, 2)]
        groups.append([int(np.ravel_multi_index(member, sizes)) for member in members])
    return groups


def shards(master_new, sent_base, rollout_base, tokens, lengths, expert_slot):
    lengths = lengths.T
    out, lengths, expert_slot = pl.pallas_call(
        encode_kernel,
        out_shape=(
            jax.ShapeDtypeStruct((32, 2, PART, BLK), jnp.bfloat16),
            jax.typeof(lengths),
            jax.typeof(expert_slot),
        ),
        in_specs=[HBM] * 4,
        out_specs=(VMEM,) * 3,
        scratch_shapes=[
            pltpu.SMEM(lengths.shape, jnp.int32),
            pltpu.VMEM((MOST, BLK, BLK), jnp.float32),
            pltpu.VMEM((MOST, BLK, BLK), jnp.bfloat16),
            pltpu.SemaphoreType.DMA((3 + 2 * MOST,)),
        ],
        compiler_params=LIMIT,
        name="encode",
    )(*(pltpu.with_memory_space_constraint(v, pltpu.HBM) for v in (lengths, expert_slot, master_new, sent_base)))
    out = exchange(out, ("zl", "x", "c", "yc"))
    (out,) = call(
        slot_kernel, "slot", [SMEM, SMEM, VMEM], [(16, 2, PART, BLK)], lengths, expert_slot, out,
        scratch=[pltpu.SMEM((2, 64), jnp.int32)],
    )
    out = lax.all_to_all(
        out, tuple(AXES), split_axis=0, concat_axis=0, tiled=True, axis_index_groups=turned_groups()
    )
    (out,) = call(spread_kernel, "spread", [VMEM], [(8, 8, 3, PART, BLK)], out)
    mine = exchange(out, ("zl", "x"))
    other = lax.ppermute(mine, "c", [(0, 1), (1, 0)])
    in_flight = lax.dot_general(
        tokens[0, 0], rollout_base, (((1,), (1,)), ((), ())), preferred_element_type=jnp.float32
    ).astype(jnp.bfloat16)[None, None]
    half = (3, HALF, rollout_base.shape[1])
    (new_mine,) = call(add_mine_kernel, "add_mine", [VMEM] * 2, [half], mine, rollout_base)
    new_weights = pl.pallas_call(
        add_other_kernel,
        out_shape=jax.typeof(rollout_base),
        in_specs=[VMEM] * 3,
        out_specs=HBM,
        scratch_shapes=[pltpu.VMEM(half, jnp.bfloat16), pltpu.SemaphoreType.DMA((6,))],
        compiler_params=LIMIT,
        name="add_other",
    )(other, rollout_base, new_mine)
    return (new_weights, in_flight)


def solution(mesh):
    fine = Mesh(mesh.devices.reshape(tuple(AXES.values())), tuple(AXES))
    group, shard = ("zl", "x", "c"), ("zh", "ya", "yb", "yc")
    placed = (
        P(shard, group, None, None),
        P(shard, group, None, None),
        P(shard, None),
        P(group, shard, None, None),
        P(),
        P(),
    )
    return jax.shard_map(
        shards,
        mesh=fine,
        in_specs=placed,
        out_specs=(P(shard, None), P(group, shard, None, None)),
        check_vma=False,
    )
```

```python
import jax
import jax.numpy as jnp
import numpy as np
from jax import lax
from jax.experimental import pallas as pl
from jax.experimental.pallas import tpu as pltpu
from jax.sharding import Mesh
from jax.sharding import PartitionSpec as P

CLIP_RATIO = 2.5
EPSILON = 1e-06

AXES = {"zl": 2, "x": 4, "c": 2, "zh": 4, "ya": 2, "yb": 2, "yc": 2}
BLK = 128
HALF = 64
PART = 16
TROWS = 12
MOST = 6
GROUPS = 16
EXPERTS = 8


def rank_of(col):
    return col ^ ((col >> 2 & 1) * 3)


class Place:
    def __init__(self):
        at = {name: lax.axis_index(name) for name in AXES}
        self.c, self.x, self.yb, self.yc = at["c"], at["x"], at["yb"], at["yc"]
        self.g = at["zl"] * 8 + at["x"] * 2 + at["c"]
        self.turn = (at["zh"] >> 1) ^ (at["zh"] & 1)
        self.col = at["zh"] * 4 + at["ya"] * 2 + at["yb"]
        self.s = 2 * self.col + at["yc"]


def encode_kernel(lengths_in, slots_in, master_in, sent_in, out, lengths_out, slots_out, lengths, master, sent, sems):
    loads = [
        pltpu.make_async_copy(lengths_in, lengths, sems.at[0]),
        pltpu.make_async_copy(lengths_in, lengths_out, sems.at[1]),
        pltpu.make_async_copy(slots_in, slots_out, sems.at[2]),
    ]
    for j in range(MOST):
        loads.append(pltpu.make_async_copy(master_in.at[0, j], master.at[j], sems.at[3 + 2 * j]))
        loads.append(pltpu.make_async_copy(sent_in.at[0, j], sent.at[j], sems.at[4 + 2 * j]))
    for load in loads:
        load.start()
    at = Place()
    loads[0].wait()
    start = jnp.int32(0)
    for n in range(GROUPS - 1):
        start += jnp.where(n < at.g, lengths[n, at.s], 0)
    for load in loads[3:]:
        load.wait()
    for j in range(MOST):
        change = master[j] - sent[j].astype(jnp.float32)
        mean = jnp.sum(change * change, axis=(0, 1), keepdims=True) * (1.0 / (BLK * BLK))
        scale = jnp.sqrt(mean + EPSILON).astype(jnp.bfloat16).astype(jnp.float32)
        encoded = jnp.clip(change / scale, -CLIP_RATIO, CLIP_RATIO).astype(jnp.bfloat16)
        value = (encoded.astype(jnp.float32) * scale).astype(jnp.bfloat16)
        r = lax.rem(start + j, TROWS)
        k, i = lax.div(r, 3), lax.rem(r, 3)
        to = (((k >> 1) + i + at.yb) & 1) * 4 + (k & 1)
        slot = 0 if j < 2 else 1 if j == 5 else i >> 1
        for n in range(8):
            peer = ((n >> 1 & 1) ^ at.turn) * 16 + (n & 1) * 8 + (n >> 2) * 2
            out[peer + to, slot] = value[n * PART : (n + 1) * PART, :]

    loads[1].wait()
    loads[2].wait()


def slot_kernel(lengths, slots, got, out, table):
    at = Place()
    for side in range(2):
        start = jnp.int32(0)
        for n in range(GROUPS):
            for j in range(MOST):
                table[side, start + j] = n * 8 + j
            start += lengths[n, 2 * at.col + side]
    odd = (at.x + at.yb) & 1
    for e in range(EXPERTS):
        p = slots[e]
        for i in range(3):
            kb = odd ^ (i & 1)
            entry = table[e // 4, (e % 4) * TROWS + 6 * kb + 3 * at.yc + i]
            slot = jnp.where((entry & 7) >= (2 if i == 2 else 5), 1, 0)
            out[rank_of(2 * p + kb), i >> 1] = got[(entry >> 3) * 2 + e // 4, slot]


def spread_kernel(got, out):
    at = Place()
    side = (at.x + at.yb) & 1
    for n in range(8):
        here, there = rank_of(2 * n + side), rank_of(2 * n + 1 - side)
        parts = (got[here, 0], got[here, 1], got[there, 0])
        for to in range(8):
            for m in range(3):
                out[to, n, m] = parts[m]


def add_rows(at, half, i, tiles, base, new):
    for n in range(4):
        rows = pl.ds(pl.multiple_of(i * BLK + half * HALF + n * PART, PART), PART)
        for col in range(16):
            cols = pl.ds(col * BLK, BLK)
            chip = 4 * ((n >> 1) ^ at.turn) + 2 * (n & 1) + ((at.yb + i + col) & 1)
            part = tiles[chip, col >> 1, (0, 2, 1)[i]].astype(jnp.float32)
            new[i, n * PART : (n + 1) * PART, cols] = (base[rows, cols].astype(jnp.float32) + part).astype(jnp.bfloat16)


def add_mine_kernel(mine, base, new):
    at = Place()
    for i in range(3):
        add_rows(at, at.c, i, mine, base, new)


def add_other_kernel(other, base, new_mine, out, new, sems):
    at = Place()
    stores = []

    def store(half, i, rows):
        first = pl.multiple_of(i * BLK + half * HALF, HALF)
        stores.append(pltpu.make_async_copy(rows.at[i], out.at[pl.ds(first, HALF)], sems.at[len(stores)]))
        stores[-1].start()

    for i in range(3):
        store(at.c, i, new_mine)
    for i in range(3):
        add_rows(at, 1 - at.c, i, other, base, new)
        store(1 - at.c, i, new)
    for started in stores:
        started.wait()


SMEM = pl.BlockSpec(memory_space=pltpu.SMEM)
VMEM = pl.BlockSpec(memory_space=pltpu.VMEM)
HBM = pl.BlockSpec(memory_space=pltpu.HBM)
LIMIT = pltpu.CompilerParams(vmem_limit_bytes=32 * 1024 * 1024)


def call(kernel, name, specs, shapes, *args, scratch=()):
    outs = tuple(jax.ShapeDtypeStruct(s, jnp.bfloat16) for s in shapes)
    return pl.pallas_call(
        kernel,
        out_shape=outs,
        in_specs=specs,
        out_specs=(VMEM,) * len(outs),
        scratch_shapes=scratch,
        compiler_params=LIMIT,
        name=name,
    )(*args)


def exchange(x, axes):
    return lax.all_to_all(x, axes, split_axis=0, concat_axis=0, tiled=True)


def turned_groups():
    sizes = tuple(AXES.values())
    groups = []
    for side, x, c, yc in np.ndindex(2, 4, 2, 2):
        group = [0] * 16
        for zh, ya, yb in np.ndindex(4, 2, 2):
            member = (side ^ (zh >> 1) ^ (zh & 1), x, c, zh, ya, yb, yc)
            group[rank_of(zh * 4 + ya * 2 + yb)] = int(np.ravel_multi_index(member, sizes))
        groups.append(group)
    return groups


def shards(master_new, sent_base, rollout_base, tokens, lengths, expert_slot):
    lengths = lengths.T
    out, lengths, expert_slot = pl.pallas_call(
        encode_kernel,
        out_shape=(
            jax.ShapeDtypeStruct((32, 2, PART, BLK), jnp.bfloat16),
            jax.typeof(lengths),
            jax.typeof(expert_slot),
        ),
        in_specs=[HBM] * 4,
        out_specs=(VMEM,) * 3,
        scratch_shapes=[
            pltpu.SMEM(lengths.shape, jnp.int32),
            pltpu.VMEM((MOST, BLK, BLK), jnp.float32),
            pltpu.VMEM((MOST, BLK, BLK), jnp.bfloat16),
            pltpu.SemaphoreType.DMA((3 + 2 * MOST,)),
        ],
        compiler_params=LIMIT,
        name="encode",
    )(*(pltpu.with_memory_space_constraint(v, pltpu.HBM) for v in (lengths, expert_slot, master_new, sent_base)))
    out = exchange(out, ("zl", "x", "c", "yc"))
    (out,) = call(
        slot_kernel, "slot", [SMEM, SMEM, VMEM], [(16, 2, PART, BLK)], lengths, expert_slot, out,
        scratch=[pltpu.SMEM((2, 64), jnp.int32)],
    )
    out = lax.all_to_all(
        out, tuple(AXES), split_axis=0, concat_axis=0, tiled=True, axis_index_groups=turned_groups()
    )
    (out,) = call(spread_kernel, "spread", [VMEM], [(8, 8, 3, PART, BLK)], out)
    mine = exchange(out, ("zl", "x"))
    other = lax.ppermute(mine, "c", [(0, 1), (1, 0)])
    in_flight = lax.dot_general(
        tokens[0, 0], rollout_base, (((1,), (1,)), ((), ())), preferred_element_type=jnp.float32
    ).astype(jnp.bfloat16)[None, None]
    half = (3, HALF, rollout_base.shape[1])
    (new_mine,) = call(add_mine_kernel, "add_mine", [VMEM] * 2, [half], mine, rollout_base)
    new_weights = pl.pallas_call(
        add_other_kernel,
        out_shape=jax.typeof(rollout_base),
        in_specs=[VMEM] * 3,
        out_specs=HBM,
        scratch_shapes=[pltpu.VMEM(half, jnp.bfloat16), pltpu.SemaphoreType.DMA((6,))],
        compiler_params=LIMIT,
        name="add_other",
    )(other, rollout_base, new_mine)
    return (new_weights, in_flight)


def solution(mesh):
    fine = Mesh(mesh.devices.reshape(tuple(AXES.values())), tuple(AXES))
    group, shard = ("zl", "x", "c"), ("zh", "ya", "yb", "yc")
    placed = (
        P(shard, group, None, None),
        P(shard, group, None, None),
        P(shard, None),
        P(group, shard, None, None),
        P(),
        P(),
    )
    return jax.shard_map(
        shards,
        mesh=fine,
        in_specs=placed,
        out_specs=(P(shard, None), P(group, shard, None, None)),
        check_vma=False,
    )
```

```python
import jax
import jax.numpy as jnp
import numpy as np
from jax import lax
from jax.experimental import pallas as pl
from jax.experimental.pallas import tpu as pltpu
from jax.sharding import Mesh
from jax.sharding import PartitionSpec as P

CLIP_RATIO = 2.5
EPSILON = 1e-06

AXES = {"zl": 2, "x": 4, "c": 2, "zh": 4, "ya": 2, "yb": 2, "yc": 2}
BLK = 128
HALF = 64
PART = 16
TROWS = 12
MOST = 6
GROUPS = 16
EXPERTS = 8


class Place:
    def __init__(self):
        at = {name: lax.axis_index(name) for name in AXES}
        self.c, self.x, self.yb, self.yc = at["c"], at["x"], at["yb"], at["yc"]
        self.g = at["zl"] * 8 + at["x"] * 2 + at["c"]
        self.turn = (at["zh"] >> 1) ^ (at["zh"] & 1)
        self.col = at["zh"] * 4 + at["ya"] * 2 + at["yb"]
        self.s = 2 * self.col + at["yc"]


def encode_kernel(lengths_in, slots_in, master_in, sent_in, out, lengths_out, slots_out, lengths, master, sent, sems):
    loads = [
        pltpu.make_async_copy(lengths_in, lengths, sems.at[0]),
        pltpu.make_async_copy(lengths_in, lengths_out, sems.at[1]),
        pltpu.make_async_copy(slots_in, slots_out, sems.at[2]),
    ]
    for j in range(MOST):
        loads.append(pltpu.make_async_copy(master_in.at[0, j], master.at[j], sems.at[3 + 2 * j]))
        loads.append(pltpu.make_async_copy(sent_in.at[0, j], sent.at[j], sems.at[4 + 2 * j]))
    for load in loads:
        load.start()
    at = Place()
    loads[0].wait()
    start = jnp.int32(0)
    for n in range(GROUPS - 1):
        start += jnp.where(n < at.g, lengths[n, at.s], 0)
    for load in loads[3:]:
        load.wait()
    for j in range(MOST):
        change = master[j] - sent[j].astype(jnp.float32)
        mean = jnp.sum(change * change, axis=(0, 1), keepdims=True) * (1.0 / (BLK * BLK))
        scale = jnp.sqrt(mean + EPSILON).astype(jnp.bfloat16).astype(jnp.float32)
        encoded = jnp.clip(change / scale, -CLIP_RATIO, CLIP_RATIO).astype(jnp.bfloat16)
        value = (encoded.astype(jnp.float32) * scale).astype(jnp.bfloat16)
        r = lax.rem(start + j, TROWS)
        k, i = lax.div(r, 3), lax.rem(r, 3)
        to = (((k >> 1) + i + at.yb) & 1) * 4 + (k & 1)
        slot = 0 if j < 2 else 1 if j == 5 else i >> 1
        for n in range(8):
            peer = ((n >> 1 & 1) ^ at.turn) * 16 + (n & 1) * 8 + (n >> 2) * 2
            out[31 - peer - to, slot] = value[n * PART : (n + 1) * PART, :]

    loads[1].wait()
    loads[2].wait()


def slot_kernel(lengths, slots, got, out, table):
    at = Place()
    for side in range(2):
        start = jnp.int32(0)
        for n in range(GROUPS):
            for j in range(MOST):
                table[side, start + j] = n * 8 + j
            start += lengths[n, 2 * at.col + side]
    odd = (at.x + at.yb) & 1
    for e in range(EXPERTS):
        p = slots[e]
        for i in range(3):
            kb = odd ^ (i & 1)
            entry = table[e // 4, (e % 4) * TROWS + 6 * kb + 3 * at.yc + i]
            slot = jnp.where((entry & 7) >= (2 if i == 2 else 5), 1, 0)
            out[15 - 2 * p - kb, i >> 1] = got[31 - (entry >> 3) * 2 - e // 4, slot]


def spread_kernel(got, out):
    at = Place()
    side = (at.x + at.yb) & 1
    for n in range(8):
        here, there = 15 - 2 * n - side, 14 - 2 * n + side
        parts = (got[here, 0], got[here, 1], got[there, 0])
        for to in range(8):
            for m in range(3):
                out[to, n, m] = parts[m]


def add_rows(at, half, i, tiles, base, new):
    for n in range(4):
        rows = pl.ds(pl.multiple_of(i * BLK + half * HALF + n * PART, PART), PART)
        for col in range(16):
            cols = pl.ds(col * BLK, BLK)
            chip = 4 * ((n >> 1) ^ at.turn) + 2 * (n & 1) + ((at.yb + i + col) & 1)
            part = tiles[7 - chip, col >> 1, (0, 2, 1)[i]].astype(jnp.float32)
            new[i, n * PART : (n + 1) * PART, cols] = (base[rows, cols].astype(jnp.float32) + part).astype(jnp.bfloat16)


def add_mine_kernel(mine, base, new):
    at = Place()
    for i in range(3):
        add_rows(at, at.c, i, mine, base, new)


def add_other_kernel(other, base, new_mine, out, new, sems):
    at = Place()
    stores = []

    def store(half, i, rows):
        first = pl.multiple_of(i * BLK + half * HALF, HALF)
        stores.append(pltpu.make_async_copy(rows.at[i], out.at[pl.ds(first, HALF)], sems.at[len(stores)]))
        stores[-1].start()

    for i in range(3):
        store(at.c, i, new_mine)
    for i in range(3):
        add_rows(at, 1 - at.c, i, other, base, new)
        store(1 - at.c, i, new)
    for started in stores:
        started.wait()


SMEM = pl.BlockSpec(memory_space=pltpu.SMEM)
VMEM = pl.BlockSpec(memory_space=pltpu.VMEM)
HBM = pl.BlockSpec(memory_space=pltpu.HBM)
LIMIT = pltpu.CompilerParams(vmem_limit_bytes=32 * 1024 * 1024)


def call(kernel, name, specs, shapes, *args, scratch=()):
    outs = tuple(jax.ShapeDtypeStruct(s, jnp.bfloat16) for s in shapes)
    return pl.pallas_call(
        kernel,
        out_shape=outs,
        in_specs=specs,
        out_specs=(VMEM,) * len(outs),
        scratch_shapes=scratch,
        compiler_params=LIMIT,
        name=name,
    )(*args)


def exchange(x, names, turn=lambda zh: 0):
    sizes = tuple(AXES.values())
    rest = [name for name in AXES if name not in names]
    groups = []
    for fixed in np.ndindex(*(AXES[name] for name in rest)):
        group = []
        for moving in np.ndindex(*(AXES[name] for name in names)):
            at = dict(zip((*rest, *names), fixed + moving))
            at["zl"] ^= turn(at["zh"])
            group.append(int(np.ravel_multi_index([at[name] for name in AXES], sizes)))
        groups.append(group[::-1])
    return lax.all_to_all(x, tuple(AXES), split_axis=0, concat_axis=0, tiled=True, axis_index_groups=groups)


def shards(master_new, sent_base, rollout_base, tokens, lengths, expert_slot):
    lengths = lengths.T
    out, lengths, expert_slot = pl.pallas_call(
        encode_kernel,
        out_shape=(
            jax.ShapeDtypeStruct((32, 2, PART, BLK), jnp.bfloat16),
            jax.typeof(lengths),
            jax.typeof(expert_slot),
        ),
        in_specs=[HBM] * 4,
        out_specs=(VMEM,) * 3,
        scratch_shapes=[
            pltpu.SMEM(lengths.shape, jnp.int32),
            pltpu.VMEM((MOST, BLK, BLK), jnp.float32),
            pltpu.VMEM((MOST, BLK, BLK), jnp.bfloat16),
            pltpu.SemaphoreType.DMA((3 + 2 * MOST,)),
        ],
        compiler_params=LIMIT,
        name="encode",
    )(*(pltpu.with_memory_space_constraint(v, pltpu.HBM) for v in (lengths, expert_slot, master_new, sent_base)))
    out = exchange(out, ("zl", "x", "c", "yc"))
    (out,) = call(
        slot_kernel, "slot", [SMEM, SMEM, VMEM], [(16, 2, PART, BLK)], lengths, expert_slot, out,
        scratch=[pltpu.SMEM((2, 64), jnp.int32)],
    )
    out = exchange(out, ("zh", "ya", "yb"), lambda zh: (zh >> 1) ^ (zh & 1))
    (out,) = call(spread_kernel, "spread", [VMEM], [(8, 8, 3, PART, BLK)], out)
    mine = exchange(out, ("zl", "x"))
    other = lax.ppermute(mine, "c", [(0, 1), (1, 0)])
    in_flight = lax.dot_general(
        tokens[0, 0], rollout_base, (((1,), (1,)), ((), ())), preferred_element_type=jnp.float32
    ).astype(jnp.bfloat16)[None, None]
    half = (3, HALF, rollout_base.shape[1])
    (new_mine,) = call(add_mine_kernel, "add_mine", [VMEM] * 2, [half], mine, rollout_base)
    new_weights = pl.pallas_call(
        add_other_kernel,
        out_shape=jax.typeof(rollout_base),
        in_specs=[VMEM] * 3,
        out_specs=HBM,
        scratch_shapes=[pltpu.VMEM(half, jnp.bfloat16), pltpu.SemaphoreType.DMA((6,))],
        compiler_params=LIMIT,
        name="add_other",
    )(other, rollout_base, new_mine)
    return (new_weights, in_flight)


def solution(mesh):
    fine = Mesh(mesh.devices.reshape(tuple(AXES.values())), tuple(AXES))
    group, shard = ("zl", "x", "c"), ("zh", "ya", "yb", "yc")
    placed = (
        P(shard, group, None, None),
        P(shard, group, None, None),
        P(shard, None),
        P(group, shard, None, None),
        P(),
        P(),
    )
    return jax.shard_map(
        shards,
        mesh=fine,
        in_specs=placed,
        out_specs=(P(shard, None), P(group, shard, None, None)),
        check_vma=False,
    )
```

```python
import jax
import jax.numpy as jnp
import numpy as np
from jax import lax
from jax.experimental import pallas as pl
from jax.experimental.pallas import tpu as pltpu
from jax.sharding import Mesh
from jax.sharding import PartitionSpec as P

CLIP_RATIO = 2.5
EPSILON = 1e-06

AXES = {"zl": 2, "x": 4, "c": 2, "zh": 4, "ya": 2, "yb": 2, "yc": 2}
BLK = 128
HALF = 64
PART = 16
TROWS = 12
MOST = 6
GROUPS = 16
EXPERTS = 8


class Place:
    def __init__(self):
        at = {name: lax.axis_index(name) for name in AXES}
        self.c, self.x, self.yb, self.yc = at["c"], at["x"], at["yb"], at["yc"]
        self.g = at["zl"] * 8 + at["x"] * 2 + at["c"]
        self.turn = (at["zh"] >> 1) ^ (at["zh"] & 1)
        self.col = at["zh"] * 4 + at["ya"] * 2 + at["yb"]
        self.s = 2 * self.col + at["yc"]


def encode_kernel(lengths_in, slots_in, master_in, sent_in, out, lengths_out, slots_out, lengths, master, sent, sems):
    loads = [
        pltpu.make_async_copy(lengths_in, lengths, sems.at[0]),
        pltpu.make_async_copy(lengths_in, lengths_out, sems.at[1]),
        pltpu.make_async_copy(slots_in, slots_out, sems.at[2]),
    ]
    for j in range(MOST):
        loads.append(pltpu.make_async_copy(master_in.at[0, j], master.at[j], sems.at[3 + 2 * j]))
        loads.append(pltpu.make_async_copy(sent_in.at[0, j], sent.at[j], sems.at[4 + 2 * j]))
    for load in loads:
        load.start()
    at = Place()
    loads[0].wait()
    start = jnp.int32(0)
    for n in range(GROUPS - 1):
        start += jnp.where(n < at.g, lengths[n, at.s], 0)
    for load in loads[3:]:
        load.wait()
    for j in range(MOST):
        change = master[j] - sent[j].astype(jnp.float32)
        mean = jnp.sum(change * change, axis=(0, 1), keepdims=True) * (1.0 / (BLK * BLK))
        scale = jnp.sqrt(mean + EPSILON).astype(jnp.bfloat16).astype(jnp.float32)
        encoded = jnp.clip(change / scale, -CLIP_RATIO, CLIP_RATIO).astype(jnp.bfloat16)
        value = (encoded.astype(jnp.float32) * scale).astype(jnp.bfloat16)
        r = lax.rem(start + j, TROWS)
        k, i = lax.div(r, 3), lax.rem(r, 3)
        to = (((k >> 1) + i + at.yb) & 1) + (k & 1) * 8
        slot = 0 if j < 2 else 1 if j == 5 else i >> 1
        for n in range(8):
            peer = (n >> 2) * 16 + ((n >> 1 & 1) ^ at.turn) * 4 + (n & 1) * 2
            out[31 - peer - to, slot] = value[n * PART : (n + 1) * PART, :]

    loads[1].wait()
    loads[2].wait()


def slot_kernel(lengths, slots, got, out, table):
    at = Place()
    for side in range(2):
        start = jnp.int32(0)
        for n in range(GROUPS):
            for j in range(MOST):
                table[side, start + j] = n * 8 + j
            start += lengths[n, 2 * at.col + side]
    odd = (at.x + at.yb) & 1
    for e in range(EXPERTS):
        p = slots[e]
        for i in range(3):
            kb = odd ^ (i & 1)
            entry = table[e // 4, (e % 4) * TROWS + 6 * kb + 3 * at.yc + i]
            slot = jnp.where((entry & 7) >= (2 if i == 2 else 5), 1, 0)
            out[15 - 2 * p - kb, i >> 1] = got[31 - (entry >> 3 & 1) * 16 - e // 4 * 8 - (entry >> 4), slot]


def spread_kernel(got, out):
    at = Place()
    side = (at.x + at.yb) & 1
    for n in range(8):
        here, there = 15 - 2 * n - side, 14 - 2 * n + side
        parts = (got[here, 0], got[here, 1], got[there, 0])
        for to in range(8):
            for m in range(3):
                out[to, n, m] = parts[m]


def add_rows(at, half, i, tiles, base, new):
    for n in range(4):
        rows = pl.ds(pl.multiple_of(i * BLK + half * HALF + n * PART, PART), PART)
        for col in range(16):
            cols = pl.ds(col * BLK, BLK)
            chip = 4 * ((n >> 1) ^ at.turn) + 2 * (n & 1) + ((at.yb + i + col) & 1)
            part = tiles[7 - chip, col >> 1, (0, 2, 1)[i]].astype(jnp.float32)
            new[i, n * PART : (n + 1) * PART, cols] = (base[rows, cols].astype(jnp.float32) + part).astype(jnp.bfloat16)


def add_mine_kernel(mine, base, new):
    at = Place()
    for i in range(3):
        add_rows(at, at.c, i, mine, base, new)


def add_other_kernel(other, base, new_mine, out, new, sems):
    at = Place()
    stores = []

    def store(half, i, rows):
        first = pl.multiple_of(i * BLK + half * HALF, HALF)
        stores.append(pltpu.make_async_copy(rows.at[i], out.at[pl.ds(first, HALF)], sems.at[len(stores)]))
        stores[-1].start()

    for i in range(3):
        store(at.c, i, new_mine)
    for i in range(3):
        add_rows(at, 1 - at.c, i, other, base, new)
        store(1 - at.c, i, new)
    for started in stores:
        started.wait()


SMEM = pl.BlockSpec(memory_space=pltpu.SMEM)
VMEM = pl.BlockSpec(memory_space=pltpu.VMEM)
HBM = pl.BlockSpec(memory_space=pltpu.HBM)
LIMIT = pltpu.CompilerParams(vmem_limit_bytes=32 * 1024 * 1024)


def call(kernel, name, specs, shapes, *args, scratch=()):
    outs = tuple(jax.ShapeDtypeStruct(s, jnp.bfloat16) for s in shapes)
    return pl.pallas_call(
        kernel,
        out_shape=outs,
        in_specs=specs,
        out_specs=(VMEM,) * len(outs),
        scratch_shapes=scratch,
        compiler_params=LIMIT,
        name=name,
    )(*args)


def exchange(x, names, turn=lambda zh: 0):
    sizes = tuple(AXES.values())
    rest = [name for name in AXES if name not in names]
    groups = []
    for fixed in np.ndindex(*(AXES[name] for name in rest)):
        group = []
        for moving in np.ndindex(*(AXES[name] for name in names)):
            at = dict(zip((*rest, *names), fixed + moving))
            at["zl"] ^= turn(at["zh"])
            group.append(int(np.ravel_multi_index([at[name] for name in AXES], sizes)))
        groups.append(group[::-1])
    return lax.all_to_all(x, tuple(AXES), split_axis=0, concat_axis=0, tiled=True, axis_index_groups=groups)


def shards(master_new, sent_base, rollout_base, tokens, lengths, expert_slot):
    lengths = lengths.T
    out, lengths, expert_slot = pl.pallas_call(
        encode_kernel,
        out_shape=(
            jax.ShapeDtypeStruct((32, 2, PART, BLK), jnp.bfloat16),
            jax.typeof(lengths),
            jax.typeof(expert_slot),
        ),
        in_specs=[HBM] * 4,
        out_specs=(VMEM,) * 3,
        scratch_shapes=[
            pltpu.SMEM(lengths.shape, jnp.int32),
            pltpu.VMEM((MOST, BLK, BLK), jnp.float32),
            pltpu.VMEM((MOST, BLK, BLK), jnp.bfloat16),
            pltpu.SemaphoreType.DMA((3 + 2 * MOST,)),
        ],
        compiler_params=LIMIT,
        name="encode",
    )(*(pltpu.with_memory_space_constraint(v, pltpu.HBM) for v in (lengths, expert_slot, master_new, sent_base)))
    out = exchange(out, ("c", "yc", "zl", "x"))
    (out,) = call(
        slot_kernel, "slot", [SMEM, SMEM, VMEM], [(16, 2, PART, BLK)], lengths, expert_slot, out,
        scratch=[pltpu.SMEM((2, 64), jnp.int32)],
    )
    out = exchange(out, ("zh", "ya", "yb"), lambda zh: (zh >> 1) ^ (zh & 1))
    (out,) = call(spread_kernel, "spread", [VMEM], [(8, 8, 3, PART, BLK)], out)
    mine = exchange(out, ("zl", "x"))
    other = lax.ppermute(mine, "c", [(0, 1), (1, 0)])
    in_flight = lax.dot_general(
        tokens[0, 0], rollout_base, (((1,), (1,)), ((), ())), preferred_element_type=jnp.float32
    ).astype(jnp.bfloat16)[None, None]
    half = (3, HALF, rollout_base.shape[1])
    (new_mine,) = call(add_mine_kernel, "add_mine", [VMEM] * 2, [half], mine, rollout_base)
    new_weights = pl.pallas_call(
        add_other_kernel,
        out_shape=jax.typeof(rollout_base),
        in_specs=[VMEM] * 3,
        out_specs=HBM,
        scratch_shapes=[pltpu.VMEM(half, jnp.bfloat16), pltpu.SemaphoreType.DMA((6,))],
        compiler_params=LIMIT,
        name="add_other",
    )(other, rollout_base, new_mine)
    return (new_weights, in_flight)


def solution(mesh):
    fine = Mesh(mesh.devices.reshape(tuple(AXES.values())), tuple(AXES))
    group, shard = ("zl", "x", "c"), ("zh", "ya", "yb", "yc")
    placed = (
        P(shard, group, None, None),
        P(shard, group, None, None),
        P(shard, None),
        P(group, shard, None, None),
        P(),
        P(),
    )
    return jax.shard_map(
        shards,
        mesh=fine,
        in_specs=placed,
        out_specs=(P(shard, None), P(group, shard, None, None)),
        check_vma=False,
    )
```
